32 devices in a mesh: grp: 2 (over y), pair: 4 (over z), occ: 2 (over x), rep: 2 (over core).
Axes of the slice: x: 2, y: 2, z: 4, core: 2. Of those that a mesh axis runs over, the one named last changes fastest.
Arguments:
- pair_tiles: bfloat16 [192, 16, 4096], P(('grp', 'pair'), ('occ', 'rep')), parts along dimension 0, may hold values from -6 to 6
- block_list: int32 [192, 2], P(('grp', 'pair')), parts along dimension 0, may hold values from 0 to 79, as said below
- owner_blocks: int32 [8, 4], P('grp'), parts along dimension 0, may hold values from 0 to 15, as said below
- coulomb_metric: bfloat16 [2048, 1024], P(('grp', 'pair'), ('occ', 'rep')), parts along dimension 0, may hold values from -0.5 to 0.5
Outputs:
- contracted: bfloat16 [192, 16, 4096], P(('grp', 'pair'), ('occ', 'rep')), parts along dimension 0
- pol_blocks: float32 [192, 4096], P(('grp', 'pair', 'occ', 'rep')), parts along dimension 0
The draws below stay inside these ranges and needn't reach their ends.
There are 2 independent parts, one for each index of `grp`. The reference program is written for one: setup_inputs(seed, part) draws one part's arguments, and reference() takes and returns one part's arrays. A program takes and returns all parts, laid end to end along the dimension named above; each array names one. Nothing has to cross between parts.
Inputs may be any that keep to these rules, and one draw needn't show every extreme that they name: owner_blocks holds every auxiliary block once. `block_list`: column 0 is a nu-block: tiles on index j of pair have nu-blocks in j * 20 to (j + 1) * 20 - 1. Column 1 is an auxiliary block. Tiles come in pairs with one nu-block and two different auxiliary blocks; no other tile has that nu-block. At most 12 tiles of one index of pair have auxiliary blocks of one owner, and one owner gets exactly 12 from every index of pair.
All inputs are finite; a program needn't handle non-finite values.
Results may differ from the reference program's by a relative error of at most 0.0075.
Values may be sent and summed in bfloat16 or wider, within the bound.
A program may use at most 64 MiB of HBM per device.

```python
import jax
import jax.numpy as jnp
from jax import lax

BLK = 64
PBD = 4
NBD = 20
SLOTS = 24
OCC = 16
NAB = 16
AUX = 1024
TILES = 96
N_PAIR = 4


def shared_layout(key):
    owners_table = jax.random.permutation(jax.random.fold_in(key, 11), PBD * N_PAIR).astype(jnp.int32).reshape(N_PAIR, PBD)
    hot_owner = jax.random.randint(jax.random.fold_in(key, 12), (), 0, N_PAIR).astype(jnp.int32)
    capacity = max(2, 2 * SLOTS // N_PAIR)
    groups = SLOTS // 2

    def one_source(source):
        source_key = jax.random.fold_in(jax.random.fold_in(key, 13), source)
        key_others, key_nu, key_first, key_second, key_shuffle = jax.random.split(source_key, 5)
        others = (hot_owner + 1 + jax.random.permutation(key_others, N_PAIR - 1).astype(jnp.int32)) % N_PAIR
        steps = jnp.arange(SLOTS, dtype=jnp.int32)
        destination = jnp.where(steps < capacity, hot_owner, others[(steps - capacity) % (N_PAIR - 1)])
        nu_raw = jax.random.permutation(key_nu, NBD).astype(jnp.int32)
        nu_perm = (nu_raw + (NBD - 1 - nu_raw[0])) % NBD
        group_nu = source * NBD + nu_perm[jnp.arange(groups, dtype=jnp.int32) % NBD]
        nu_block = jnp.repeat(group_nu, 2)
        first_local = jax.random.randint(key_first, (groups,), 0, PBD).astype(jnp.int32)
        second_local = (first_local + jax.random.randint(key_second, (groups,), 1, PBD).astype(jnp.int32)) % PBD
        local = jnp.stack([first_local, second_local], axis=1).reshape(SLOTS)
        aux_block = owners_table[destination, local]
        listed = jnp.stack([nu_block, aux_block], axis=1)
        shuffle = jax.random.permutation(key_shuffle, SLOTS)
        return listed[shuffle]
    lists = jax.vmap(one_source)(jnp.arange(N_PAIR, dtype=jnp.int32))
    return (owners_table, lists.reshape(N_PAIR * SLOTS, 2).astype(jnp.int32))


def draw_block_list(key, part):
    owners_table, lists = shared_layout(key)
    return lists


def draw_owner_blocks(key, part):
    owners_table, lists = shared_layout(key)
    return owners_table


def level_of(key, shape, cuts, least, largest):
    factor_of = 1.0
    for dim, blocks in cuts:
        draws = jax.random.uniform(jax.random.fold_in(jax.random.fold_in(key, 6), dim), (blocks,), jnp.float32, least / len(cuts), largest / len(cuts))
        factor_of = factor_of * jnp.repeat(jnp.exp(draws), shape[dim] // blocks).reshape((-1,) + (1,) * (len(shape) - 1 - dim))
    return factor_of


def scatter_about(key, extent, deviation, reach, shards=(), kind=jnp.bfloat16):
    level = level_of(key, extent, shards, -0.22, 0.18) if shards else 1.0
    result = jax.random.normal(key, extent, jnp.float32) * deviation * level
    return jnp.minimum(jnp.maximum(result, -reach), reach).astype(kind)


def setup_inputs(seed: int = 0, part: int = 0) -> dict:
    key_of = jax.random.split(jax.random.key(seed), 5)
    part_splits = jax.random.split(jax.random.fold_in(key_of[4], part), 5)
    pair_tiles = scatter_about(part_splits[0], (TILES, OCC, BLK * BLK), 1.0, 6.0, ((0, 4), (1, 4)))
    block_list = draw_block_list(jax.random.fold_in(jax.random.fold_in(key_of[4], part), 71), part)
    owner_blocks = draw_owner_blocks(jax.random.fold_in(jax.random.fold_in(key_of[4], part), 71), part)
    coulomb_metric = scatter_about(part_splits[3], (N_PAIR * PBD * BLK, AUX), (2 * BLK) ** -0.5, 0.5, ((0, 4), (1, 4)))
    return dict(pair_tiles=pair_tiles, block_list=block_list, owner_blocks=owner_blocks, coulomb_metric=coulomb_metric)


def reference(pair_tiles, block_list, owner_blocks, coulomb_metric):
    occ_rows = pair_tiles.shape[1]
    row_count = occ_rows * BLK
    nu_block = block_list[:, 0]
    aux_block = block_list[:, 1]
    matched = (owner_blocks[None, :, :] == aux_block[:, None, None]).astype(jnp.int32)
    owner_index = jnp.sum(matched * jnp.arange(N_PAIR, dtype=jnp.int32)[None, :, None], axis=(1, 2)).astype(jnp.int32)
    local_index = jnp.sum(matched * jnp.arange(PBD, dtype=jnp.int32)[None, None, :], axis=(1, 2)).astype(jnp.int32)
    metric_five = coulomb_metric.reshape(N_PAIR, PBD, BLK, NAB, BLK)

    def one_device(device):
        base = (device * SLOTS).astype(jnp.int32)
        tiles_here = lax.dynamic_slice_in_dim(pair_tiles, base, SLOTS, 0).reshape(SLOTS, row_count, BLK).astype(jnp.float32)
        nu_here = lax.dynamic_slice_in_dim(nu_block, base, SLOTS, 0)
        aux_here = lax.dynamic_slice_in_dim(aux_block, base, SLOTS, 0)
        owner_here = lax.dynamic_slice_in_dim(owner_index, base, SLOTS, 0)
        local_here = lax.dynamic_slice_in_dim(local_index, base, SLOTS, 0)
        position = jnp.arange(SLOTS, dtype=jnp.int32)
        same_nu = (nu_here[:, None] == nu_here[None, :]) & (position[:, None] != position[None, :])
        partner = jnp.sum(same_nu.astype(jnp.int32) * position[None, :], axis=1).astype(jnp.int32)
        partner_aux = aux_here[partner]
        self_blocks = metric_five[owner_here, local_here, :, aux_here, :].astype(jnp.float32)
        other_blocks = metric_five[owner_here, local_here, :, partner_aux, :].astype(jnp.float32)
        self_prod = jnp.einsum("trc,tcd->trd", tiles_here, self_blocks, precision=lax.Precision.HIGHEST).astype(jnp.bfloat16)
        other_prod = jnp.einsum("trc,tcd->trd", tiles_here, other_blocks, precision=lax.Precision.HIGHEST).astype(jnp.bfloat16)
        total = self_prod.astype(jnp.float32) + other_prod[partner].astype(jnp.float32)
        rounded = total.astype(jnp.bfloat16)
        widened = lax.optimization_barrier(rounded).astype(jnp.float32)
        pol_here = jnp.einsum("srp,srq->spq", widened, widened, precision=lax.Precision.HIGHEST).reshape(SLOTS, BLK * BLK)
        return rounded.reshape(SLOTS, occ_rows, BLK * BLK), pol_here

    contracted, pol_blocks = lax.map(one_device, jnp.arange(N_PAIR, dtype=jnp.int32))
    contracted = contracted.reshape(N_PAIR * SLOTS, occ_rows, BLK * BLK)
    pol_blocks = pol_blocks.reshape(N_PAIR * SLOTS, BLK * BLK)
    return contracted, pol_blocks
```

```python
import functools

import jax
import jax.numpy as jnp
from jax import lax
from jax.experimental import pallas as pl
from jax.experimental.pallas import tpu as pltpu
from jax.sharding import PartitionSpec as P

BLK = 64
PBD = 4
LANES = 128
MESH = pl.DeviceIdType.MESH
GATHER_LIMIT = 8 << 20


def block_exchange(pair_tiles, block_list, owner_blocks, coulomb_metric):
    slots, occ_rows = pair_tiles.shape[:2]
    rows = occ_rows * BLK
    pairs = lax.axis_size("pair")
    me = lax.axis_index("pair")
    capacity = max(2, 2 * slots // pairs)
    strip = lax.all_gather(coulomb_metric, ("occ", "rep"), axis=1, tiled=True)
    lists = lax.all_gather(block_list, "pair", axis=0, tiled=False)
    nu, aux = lists[:, :, 0], lists[:, :, 1]
    matched = (owner_blocks[None, None] == aux[:, :, None, None]).astype(jnp.int32)
    owner = jnp.sum(matched * jnp.arange(pairs, dtype=jnp.int32)[:, None], axis=(2, 3))
    local = jnp.sum(matched * jnp.arange(PBD, dtype=jnp.int32)[None, :], axis=(2, 3))
    position = jnp.arange(slots, dtype=jnp.int32)
    same_nu = (
        (nu[:, :, None] == nu[:, None, :]) & (position[:, None] != position[None, :])
    ).astype(jnp.int32)
    partner = jnp.sum(same_nu * position, axis=2)
    partner_aux = jnp.sum(same_nu * aux[:, None, :], axis=2)
    earlier = (owner[:, :, None] == owner[:, None, :]) & (position[None, :] < position[:, None])
    rank = jnp.sum(earlier.astype(jnp.int32), axis=2)
    chosen = (
        (owner == me)[:, None, :] & (rank[:, None, :] == jnp.arange(capacity)[None, :, None])
    ).astype(jnp.int32)
    send_local = jnp.sum(chosen * local[:, None, :], axis=2)
    send_aux = jnp.sum(chosen * aux[:, None, :], axis=2)
    send_partner = jnp.sum(chosen * partner_aux[:, None, :], axis=2)
    blocks = strip.reshape(PBD, BLK, -1, BLK).transpose(0, 2, 1, 3)
    send = jnp.stack([blocks[send_local, send_aux], blocks[send_local, send_partner]], axis=2)
    got = lax.all_to_all(send, "pair", split_axis=0, concat_axis=0, tiled=True)
    got = got.reshape(pairs * capacity, 2, BLK, BLK)
    mine = got[owner[me] * capacity + rank[me]]
    tiles = pair_tiles.reshape(slots, rows, BLK)
    products = jnp.einsum(
        "trc,tkcd->tkrd", tiles, mine, preferred_element_type=jnp.float32
    ).astype(jnp.bfloat16)
    total = products[:, 0].astype(jnp.float32) + products[partner[me], 1].astype(jnp.float32)
    rounded = total.astype(jnp.bfloat16)
    pol = jnp.einsum("srp,srq->spq", rounded, rounded, preferred_element_type=jnp.float32)
    pol = pol.reshape(slots, BLK * BLK).astype(jnp.bfloat16)
    pol = lax.psum_scatter(pol, ("occ", "rep"), scatter_dimension=0, tiled=True)
    return rounded.reshape(slots, occ_rows, BLK * BLK), pol.astype(jnp.float32)


def fused_kernel(
    pairs,
    n_occ,
    slots,
    lists,
    owners,
    tiles_hbm,
    metric_hbm,
    out_hbm,
    pol_ref,
    held,
    tiles,
    out,
    pol_send,
    pol_got,
    spread,
    place,
    mate,
    local_sem,
    tiles_sem,
    out_sem,
    right_send,
    left_send,
    line_got,
    x_send,
    x_got,
    core_send,
    core_got,
    pol_out_sem,
    pol_in_sem,
):
    j = lax.axis_index("pair")
    occ = lax.axis_index("occ")
    rep = lax.axis_index("rep")
    plane = 2 * n_occ
    me = occ * 2 + rep
    halves = held.shape[3]
    per_dev = slots // plane
    packs = per_dev // 2
    other_x = {"occ": 1 - occ}
    other_core = {"rep": 1 - rep}
    other_both = {"occ": 1 - occ, "rep": 1 - rep}

    load_metric = [
        pltpu.make_async_copy(
            metric_hbm.at[k * BLK : (k + 1) * BLK, h * LANES : (h + 1) * LANES],
            held.at[j, me, k, h],
            local_sem.at[k, h],
        )
        for k in range(PBD)
        for h in range(halves)
    ]
    for copy in load_metric:
        copy.start()
    load_tiles = pltpu.make_async_copy(tiles_hbm, tiles, tiles_sem)
    load_tiles.start()

    barrier = pltpu.get_barrier_semaphore()

    def greet(device):
        pl.semaphore_signal(barrier, inc=1, device_id=device, device_id_type=MESH)

    greet(other_x)
    greet(other_core)
    greet(other_both)

    @pl.when(j > 0)
    def _():
        greet({"pair": j - 1})

    @pl.when(j < pairs - 1)
    def _():
        greet({"pair": j + 1})

    inner = (j > 0) & (j < pairs - 1)

    @pl.when(inner)
    def _():
        pl.semaphore_wait(barrier, 5)

    @pl.when(jnp.logical_not(inner))
    def _():
        pl.semaphore_wait(barrier, 4)

    for copy in load_metric:
        copy.wait()

    def right(o):
        return pltpu.make_async_remote_copy(
            held.at[o, me], held.at[o, me], right_send.at[o], line_got.at[o], {"pair": j + 1}, MESH
        )

    def left(o):
        return pltpu.make_async_remote_copy(
            held.at[o, me], held.at[o, me], left_send.at[o], line_got.at[o], {"pair": j - 1}, MESH
        )

    def across(o):
        return pltpu.make_async_remote_copy(
            held.at[o, me], held.at[o, me], x_send.at[o], x_got.at[o], other_x, MESH
        )

    def arrived_x(o):
        col = (1 - occ) * 2 + rep
        return pltpu.make_async_remote_copy(
            held.at[o, col], held.at[o, col], x_send.at[o], x_got.at[o], other_x, MESH
        )

    def to_core(o, which):
        col = which * 2 + rep
        return pltpu.make_async_remote_copy(
            held.at[o, col],
            held.at[o, col],
            core_send.at[o, which],
            core_got.at[o, which],
            other_core,
            MESH,
        )

    def from_core(o, which):
        col = which * 2 + 1 - rep
        return pltpu.make_async_remote_copy(
            held.at[o, col],
            held.at[o, col],
            core_send.at[o, which],
            core_got.at[o, which],
            other_core,
            MESH,
        )

    @pl.when(j < pairs - 1)
    def _():
        right(j).start()

    @pl.when(j > 0)
    def _():
        left(j).start()

    across(j).start()
    to_core(j, occ).start()

    def find(s, carry):
        aux = lists[1, s]
        nu = lists[0, s]
        where_ = jnp.int32(0)
        for k in range(pairs * PBD):
            where_ = jnp.where(owners[k // PBD, k % PBD] == aux, k, where_)
        place[s] = where_
        other = jnp.int32(0)
        for t in range(slots):
            other = jnp.where((lists[0, t] == nu) & (s != t), t, other)
        mate[s] = other
        return carry

    lax.fori_loop(0, slots, find, 0)

    def from_x(o):
        arrived_x(o).wait_recv()
        to_core(o, 1 - occ).start()

    from_x_levels = [[j]]
    for d in range(1, pairs):
        lo, hi = j - d, j + d

        @pl.when(lo >= 0)
        def _(lo=lo):
            right(lo).wait_recv()

            @pl.when(j < pairs - 1)
            def _():
                right(lo).start()

            across(lo).start()
            to_core(lo, occ).start()

        @pl.when(hi < pairs)
        def _(hi=hi):
            left(hi).wait_recv()

            @pl.when(j > 0)
            def _():
                left(hi).start()

            across(hi).start()
            to_core(hi, occ).start()

        if d == 1:
            from_x(j)
        else:
            for o in (j - d + 1, j + d - 1):

                @pl.when((o >= 0) & (o < pairs))
                def _(o=o):
                    from_x(o)

    for o in (j - pairs + 1, j + pairs - 1):

        @pl.when((o >= 0) & (o < pairs))
        def _(o=o):
            from_x(o)

    load_tiles.wait()

    def settle(o, carry):
        from_core(o, 0).wait_recv()
        from_core(o, 1).wait_recv()
        to_core(o, 0).wait_send()
        to_core(o, 1).wait_send()
        across(o).wait_send()

        @pl.when((o <= j) & (j < pairs - 1))
        def _():
            right(o).wait_send()

        @pl.when((o >= j) & (j > 0))
        def _():
            left(o).wait_send()

        return carry

    lax.fori_loop(0, pairs, settle, 0)

    lane = lax.broadcasted_iota(jnp.int32, (BLK, LANES), 1)
    low = lane < BLK

    def weights(row, col):
        half = col // 2
        x = held[row // PBD, half // halves, row % PBD, half % halves].astype(jnp.float32)
        turned = pltpu.roll(x, BLK, 1)
        even = jnp.full((BLK, LANES), col % 2, jnp.int32) == 0
        first = jnp.where(low, jnp.where(even, x, turned), 0.0)
        second = jnp.where(low, 0.0, jnp.where(even, turned, x))
        return jnp.concatenate([first, second], axis=0).astype(jnp.bfloat16)

    def contract(s):
        t = mate[s]
        col = lists[1, s]
        w = jnp.concatenate([weights(place[s], col), weights(place[t], col)], axis=0)
        a = jnp.concatenate([tiles[s], tiles[t]], axis=1)
        c = jnp.dot(a, w, preferred_element_type=jnp.float32).astype(jnp.bfloat16)
        out[s] = c
        return lax.dot_general(c, c, (((0,), (0,)), ((), ())), preferred_element_type=jnp.float32)

    def store_out(who, index):
        span = pl.ds(who * per_dev, per_dev)
        return pltpu.make_async_copy(out.at[span], out_hbm.at[span], out_sem.at[index])

    def send_pol(index, who, device):
        return pltpu.make_async_remote_copy(
            pol_send.at[who],
            pol_got.at[index],
            pol_out_sem.at[index],
            pol_in_sem.at[index],
            device,
            MESH,
        )

    routes = (
        (((1 - occ) * 2 + 1 - rep), other_both),
        (((1 - occ) * 2 + rep), other_x),
        ((occ * 2 + 1 - rep), other_core),
        (me, None),
    )
    for index, (who, device) in enumerate(routes):
        def pack(m, carry, who=who):
            s = who * per_dev + 2 * m
            g0 = contract(s)
            g1 = contract(s + 1)
            u = jnp.where(low, g0[:BLK], g1[BLK:])
            v = jnp.where(low, g1[:BLK], g0[BLK:])
            pol_send[who, m] = (u + pltpu.roll(v, BLK, 1)).astype(jnp.bfloat16)
            return carry

        lax.fori_loop(0, packs, pack, 0)
        if device is not None:
            send_pol(index, who, device).start()
        store_out(who, index).start()

    for index, (who, device) in enumerate(routes[:-1]):
        send_pol(index, who, device).wait()
    for m in range(packs):
        total = pol_send[me, m].astype(jnp.float32)
        for index in range(plane - 1):
            total = total + pol_got[index, m].astype(jnp.float32)
        spread[m * BLK : (m + 1) * BLK, :] = total
    even = spread[pl.ds(0, packs * BLK // 2, stride=2), :]
    odd = spread[pl.ds(1, packs * BLK // 2, stride=2), :]
    half = lax.broadcasted_iota(jnp.int32, even.shape, 1) < BLK
    first = jnp.where(half, even, pltpu.roll(odd, BLK, 1))
    second = jnp.where(half, pltpu.roll(even, BLK, 1), odd)
    rows = BLK // 2
    for m in range(packs):
        pol_ref[(2 * m) * rows : (2 * m + 1) * rows, :] = first[m * rows : (m + 1) * rows]
        pol_ref[(2 * m + 1) * rows : (2 * m + 2) * rows, :] = second[m * rows : (m + 1) * rows]
    for index, (who, _) in enumerate(routes):
        store_out(who, index).wait()


def fused(pair_tiles, block_list, owner_blocks, coulomb_metric):
    slots, occ_rows, merged = pair_tiles.shape
    pairs = lax.axis_size("pair")
    n_occ = lax.axis_size("occ")
    plane = n_occ * lax.axis_size("rep")
    groups = merged // LANES
    tile_rows = occ_rows * groups
    per_dev = slots // plane
    width = coulomb_metric.shape[1]
    flat = (
        pair_tiles.reshape(slots, occ_rows, groups, LANES)
        .transpose(0, 2, 1, 3)
        .reshape(slots, tile_rows, LANES)
    )
    dma = pltpu.SemaphoreType.DMA
    out, pol = pl.pallas_call(
        functools.partial(fused_kernel, pairs, n_occ, slots),
        out_shape=(
            jax.ShapeDtypeStruct((slots, tile_rows, LANES), jnp.bfloat16),
            jax.ShapeDtypeStruct((per_dev * merged // LANES, LANES), jnp.float32),
        ),
        in_specs=[
            pl.BlockSpec(memory_space=pltpu.SMEM),
            pl.BlockSpec(memory_space=pltpu.SMEM),
            pl.BlockSpec(memory_space=pl.ANY),
            pl.BlockSpec(memory_space=pl.ANY),
        ],
        out_specs=(
            pl.BlockSpec(memory_space=pl.ANY),
            pl.BlockSpec(memory_space=pltpu.VMEM),
        ),
        scratch_shapes=[
            pltpu.VMEM((pairs, plane, PBD, width // LANES, BLK, LANES), jnp.bfloat16),
            pltpu.VMEM((slots, tile_rows, LANES), jnp.bfloat16),
            pltpu.VMEM((slots, tile_rows, LANES), jnp.bfloat16),
            pltpu.VMEM((plane, per_dev // 2, BLK, LANES), jnp.bfloat16),
            pltpu.VMEM((plane - 1, per_dev // 2, BLK, LANES), jnp.bfloat16),
            pltpu.VMEM((per_dev // 2 * BLK, LANES), jnp.float32),
            pltpu.SMEM((slots,), jnp.int32),
            pltpu.SMEM((slots,), jnp.int32),
            dma((PBD, width // LANES)),
            dma,
            dma((plane,)),
            dma((pairs,)),
            dma((pairs,)),
            dma((pairs,)),
            dma((pairs,)),
            dma((pairs,)),
            dma((pairs, n_occ)),
            dma((pairs, n_occ)),
            dma((plane - 1,)),
            dma((plane - 1,)),
        ],
        compiler_params=pltpu.CompilerParams(
            collective_id=0, has_side_effects=True, vmem_limit_bytes=32 << 20
        ),
    )(block_list.T, owner_blocks, flat, coulomb_metric)
    contracted = (
        out.reshape(slots, groups, occ_rows, LANES)
        .transpose(0, 2, 1, 3)
        .reshape(slots, occ_rows, merged)
    )
    return contracted, pol.reshape(per_dev, merged)


def per_device(pair_tiles, block_list, owner_blocks, coulomb_metric):
    pairs = lax.axis_size("pair")
    plane = lax.axis_size("occ") * lax.axis_size("rep")
    gathered = coulomb_metric.size * 2 * pairs * plane
    if gathered <= GATHER_LIMIT and lax.axis_size("occ") == 2 and lax.axis_size("rep") == 2:
        return fused(pair_tiles, block_list, owner_blocks, coulomb_metric)
    return block_exchange(pair_tiles, block_list, owner_blocks, coulomb_metric)


def solution(mesh):
    placed = (
        P(("grp", "pair"), ("occ", "rep"), None),
        P(("grp", "pair"), None),
        P("grp", None),
        P(("grp", "pair"), ("occ", "rep")),
    )
    return jax.shard_map(
        per_device,
        mesh=mesh,
        in_specs=placed,
        out_specs=(
            P(("grp", "pair"), ("occ", "rep"), None),
            P(("grp", "pair", "occ", "rep"), None),
        ),
        check_vma=False,
    )
```

```python
import functools

import jax
import jax.numpy as jnp
from jax import lax
from jax.experimental import pallas as pl
from jax.experimental.pallas import tpu as pltpu
from jax.sharding import PartitionSpec as P

BLK = 64
PBD = 4
LANES = 128
MESH = pl.DeviceIdType.MESH
GATHER_LIMIT = 8 << 20
CHUNKS = 2


def block_exchange(pair_tiles, block_list, owner_blocks, coulomb_metric):
    slots, occ_rows = pair_tiles.shape[:2]
    rows = occ_rows * BLK
    pairs = lax.axis_size("pair")
    me = lax.axis_index("pair")
    capacity = max(2, 2 * slots // pairs)
    strip = lax.all_gather(coulomb_metric, ("occ", "rep"), axis=1, tiled=True)
    lists = lax.all_gather(block_list, "pair", axis=0, tiled=False)
    nu, aux = lists[:, :, 0], lists[:, :, 1]
    matched = (owner_blocks[None, None] == aux[:, :, None, None]).astype(jnp.int32)
    owner = jnp.sum(matched * jnp.arange(pairs, dtype=jnp.int32)[:, None], axis=(2, 3))
    local = jnp.sum(matched * jnp.arange(PBD, dtype=jnp.int32)[None, :], axis=(2, 3))
    position = jnp.arange(slots, dtype=jnp.int32)
    same_nu = (
        (nu[:, :, None] == nu[:, None, :]) & (position[:, None] != position[None, :])
    ).astype(jnp.int32)
    partner = jnp.sum(same_nu * position, axis=2)
    partner_aux = jnp.sum(same_nu * aux[:, None, :], axis=2)
    earlier = (owner[:, :, None] == owner[:, None, :]) & (position[None, :] < position[:, None])
    rank = jnp.sum(earlier.astype(jnp.int32), axis=2)
    chosen = (
        (owner == me)[:, None, :] & (rank[:, None, :] == jnp.arange(capacity)[None, :, None])
    ).astype(jnp.int32)
    send_local = jnp.sum(chosen * local[:, None, :], axis=2)
    send_aux = jnp.sum(chosen * aux[:, None, :], axis=2)
    send_partner = jnp.sum(chosen * partner_aux[:, None, :], axis=2)
    blocks = strip.reshape(PBD, BLK, -1, BLK).transpose(0, 2, 1, 3)
    send = jnp.stack([blocks[send_local, send_aux], blocks[send_local, send_partner]], axis=2)
    got = lax.all_to_all(send, "pair", split_axis=0, concat_axis=0, tiled=True)
    got = got.reshape(pairs * capacity, 2, BLK, BLK)
    mine = got[owner[me] * capacity + rank[me]]
    tiles = pair_tiles.reshape(slots, rows, BLK)
    products = jnp.einsum(
        "trc,tkcd->tkrd", tiles, mine, preferred_element_type=jnp.float32
    ).astype(jnp.bfloat16)
    total = products[:, 0].astype(jnp.float32) + products[partner[me], 1].astype(jnp.float32)
    rounded = total.astype(jnp.bfloat16)
    pol = jnp.einsum("srp,srq->spq", rounded, rounded, preferred_element_type=jnp.float32)
    pol = pol.reshape(slots, BLK * BLK).astype(jnp.bfloat16)
    pol = lax.psum_scatter(pol, ("occ", "rep"), scatter_dimension=0, tiled=True)
    return rounded.reshape(slots, occ_rows, BLK * BLK), pol.astype(jnp.float32)


def fused_kernel(
    pairs,
    n_occ,
    slots,
    lists_hbm,
    owners_hbm,
    tiles_hbm,
    metric_hbm,
    out_hbm,
    pol_ref,
    held,
    tiles,
    out,
    pol_send,
    pol_got,
    spread,
    lists,
    owners,
    place,
    mate,
    local_sem,
    tiles_sem,
    table_sem,
    out_sem,
    right_send,
    left_send,
    line_got,
    x_send,
    x_got,
    core_send,
    core_got,
    pol_out_sem,
    pol_in_sem,
):
    j = lax.axis_index("pair")
    occ = lax.axis_index("occ")
    rep = lax.axis_index("rep")
    plane = 2 * n_occ
    me = occ * 2 + rep
    halves = held.shape[4]
    part = PBD // CHUNKS
    per_dev = slots // plane
    packs = per_dev // 2
    other_x = {"occ": 1 - occ}
    other_core = {"rep": 1 - rep}
    other_both = {"occ": 1 - occ, "rep": 1 - rep}

    load_metric = [
        pltpu.make_async_copy(
            metric_hbm.at[k * BLK : (k + 1) * BLK, h * LANES : (h + 1) * LANES],
            held.at[j, occ, rep, k, h],
            local_sem.at[k, h],
        )
        for k in range(PBD)
        for h in range(halves)
    ]
    for copy in load_metric:
        copy.start()
    load_tiles = pltpu.make_async_copy(tiles_hbm, tiles, tiles_sem)
    load_tiles.start()
    load_lists = pltpu.make_async_copy(lists_hbm, lists, table_sem.at[0])
    load_lists.start()
    load_owners = pltpu.make_async_copy(owners_hbm, owners, table_sem.at[1])
    load_owners.start()

    barrier = pltpu.get_barrier_semaphore()

    def greet(device):
        pl.semaphore_signal(barrier, inc=1, device_id=device, device_id_type=MESH)

    greet(other_x)
    greet(other_core)
    greet(other_both)

    @pl.when(j > 0)
    def _():
        greet({"pair": j - 1})

    @pl.when(j < pairs - 1)
    def _():
        greet({"pair": j + 1})

    inner = (j > 0) & (j < pairs - 1)

    @pl.when(inner)
    def _():
        pl.semaphore_wait(barrier, 5)

    @pl.when(jnp.logical_not(inner))
    def _():
        pl.semaphore_wait(barrier, 4)


    def chunk(o, x, core, k):
        return held.at[o, x, core, pl.ds(k * part, part)]

    def right(o, k):
        c = chunk(o, occ, rep, k)
        return pltpu.make_async_remote_copy(
            c, c, right_send.at[o], line_got.at[o, k], {"pair": j + 1}, MESH
        )

    def left(o, k):
        c = chunk(o, occ, rep, k)
        return pltpu.make_async_remote_copy(
            c, c, left_send.at[o], line_got.at[o, k], {"pair": j - 1}, MESH
        )

    def across(o, k, x=occ):
        c = chunk(o, x, rep, k)
        return pltpu.make_async_remote_copy(c, c, x_send, x_got.at[o, k], other_x, MESH)

    def to_core(o, x, k):
        c = chunk(o, x, rep, k)
        return pltpu.make_async_remote_copy(c, c, core_send, core_got, other_core, MESH)

    for k in range(CHUNKS):
        for copy in load_metric[k * part * halves : (k + 1) * part * halves]:
            copy.wait()

        @pl.when(j < pairs - 1)
        def _(k=k):
            right(j, k).start()

        @pl.when(j > 0)
        def _(k=k):
            left(j, k).start()

        across(j, k).start()
    for k in range(CHUNKS):
        to_core(j, occ, k).start()

    def find(s, carry):
        aux = lists[1, s]
        nu = lists[0, s]
        where_ = jnp.int32(0)
        for k in range(pairs * PBD):
            where_ = jnp.where(owners[k // PBD, k % PBD] == aux, k, where_)
        place[s] = where_
        other = jnp.int32(0)
        for t in range(slots):
            other = jnp.where((lists[0, t] == nu) & (s != t), t, other)
        mate[s] = other
        return carry

    load_lists.wait()
    load_owners.wait()
    lax.fori_loop(0, slots, find, 0)

    def from_x(o, k):
        across(o, k, 1 - occ).wait_recv()
        to_core(o, 1 - occ, k).start()

    for d in range(1, pairs + 1):
        for k in range(CHUNKS):
            if d < pairs:
                lo, hi = j - d, j + d

                @pl.when(lo >= 0)
                def _(lo=lo, k=k):
                    right(lo, k).wait_recv()

                    @pl.when(j < pairs - 1)
                    def _():
                        right(lo, k).start()

                    across(lo, k).start()
                    to_core(lo, occ, k).start()

                @pl.when(hi < pairs)
                def _(hi=hi, k=k):
                    left(hi, k).wait_recv()

                    @pl.when(j > 0)
                    def _():
                        left(hi, k).start()

                    across(hi, k).start()
                    to_core(hi, occ, k).start()

            if d == 1:
                from_x(j, k)
            else:
                for o in (j - d + 1, j + d - 1):

                    @pl.when((o >= 0) & (o < pairs))
                    def _(o=o, k=k):
                        from_x(o, k)

    load_tiles.wait()

    theirs = held.at[:, :, 1 - rep]
    pltpu.make_async_remote_copy(theirs, theirs, core_send, core_got, other_core, MESH).wait_recv()

    lane = lax.broadcasted_iota(jnp.int32, (BLK, LANES), 1)
    low = lane < BLK

    def weights(row, col):
        half = col // 2
        dev = half // halves
        x = held[row // PBD, dev // 2, dev % 2, row % PBD, half % halves].astype(jnp.float32)
        turned = pltpu.roll(x, BLK, 1)
        even = jnp.full((BLK, LANES), col % 2, jnp.int32) == 0
        first = jnp.where(low, jnp.where(even, x, turned), 0.0)
        second = jnp.where(low, 0.0, jnp.where(even, turned, x))
        return jnp.concatenate([first, second], axis=0).astype(jnp.bfloat16)

    def contract(s):
        t = mate[s]
        col = lists[1, s]
        w = jnp.concatenate([weights(place[s], col), weights(place[t], col)], axis=0)
        a = jnp.concatenate([tiles[s], tiles[t]], axis=1)
        c = jnp.dot(a, w, preferred_element_type=jnp.float32).astype(jnp.bfloat16)
        out[s] = c
        return lax.dot_general(c, c, (((0,), (0,)), ((), ())), preferred_element_type=jnp.float32)

    def store_out(who, index):
        span = pl.ds(who * per_dev, per_dev)
        return pltpu.make_async_copy(out.at[span], out_hbm.at[span], out_sem.at[index])

    def send_pol(index, who, device):
        return pltpu.make_async_remote_copy(
            pol_send.at[who],
            pol_got.at[index],
            pol_out_sem.at[index],
            pol_in_sem.at[index],
            device,
            MESH,
        )

    routes = (
        (((1 - occ) * 2 + 1 - rep), other_both),
        (((1 - occ) * 2 + rep), other_x),
        ((occ * 2 + 1 - rep), other_core),
        (me, None),
    )
    for index, (who, device) in enumerate(routes):
        def pack(m, carry, who=who):
            s = who * per_dev + 2 * m
            g0 = contract(s)
            g1 = contract(s + 1)
            u = jnp.where(low, g0[:BLK], g1[BLK:])
            v = jnp.where(low, g1[:BLK], g0[BLK:])
            pol_send[who, m] = (u + pltpu.roll(v, BLK, 1)).astype(jnp.bfloat16)
            return carry

        lax.fori_loop(0, packs, pack, 0)
        if device is not None:
            send_pol(index, who, device).start()
        store_out(who, index).start()

    for index, (who, device) in enumerate(routes[:-1]):
        send_pol(index, who, device).wait()
    for m in range(packs):
        total = pol_send[me, m].astype(jnp.float32)
        for index in range(plane - 1):
            total = total + pol_got[index, m].astype(jnp.float32)
        spread[m * BLK : (m + 1) * BLK, :] = total
    even = spread[pl.ds(0, packs * BLK // 2, stride=2), :]
    odd = spread[pl.ds(1, packs * BLK // 2, stride=2), :]
    half = lax.broadcasted_iota(jnp.int32, even.shape, 1) < BLK
    first = jnp.where(half, even, pltpu.roll(odd, BLK, 1))
    second = jnp.where(half, pltpu.roll(even, BLK, 1), odd)
    rows = BLK // 2
    for m in range(packs):
        pol_ref[(2 * m) * rows : (2 * m + 1) * rows, :] = first[m * rows : (m + 1) * rows]
        pol_ref[(2 * m + 1) * rows : (2 * m + 2) * rows, :] = second[m * rows : (m + 1) * rows]
    for index, (who, _) in enumerate(routes):
        store_out(who, index).wait()

    mine = held.at[:, :, rep]
    pltpu.make_async_remote_copy(mine, mine, core_send, core_got, other_core, MESH).wait_send()
    column = held.at[:, occ, rep]
    pltpu.make_async_remote_copy(column, column, x_send, x_got.at[0, 0], other_x, MESH).wait_send()

    def settle(o, carry):
        block = held.at[o, occ, rep]

        @pl.when((o <= j) & (j < pairs - 1))
        def _():
            pltpu.make_async_remote_copy(
                block, block, right_send.at[o], line_got.at[o, 0], {"pair": j + 1}, MESH
            ).wait_send()

        @pl.when((o >= j) & (j > 0))
        def _():
            pltpu.make_async_remote_copy(
                block, block, left_send.at[o], line_got.at[o, 0], {"pair": j - 1}, MESH
            ).wait_send()

        return carry

    lax.fori_loop(0, pairs, settle, 0)


def fused(pair_tiles, block_list, owner_blocks, coulomb_metric):
    slots, occ_rows, merged = pair_tiles.shape
    pairs = lax.axis_size("pair")
    n_occ = lax.axis_size("occ")
    plane = n_occ * lax.axis_size("rep")
    groups = merged // LANES
    tile_rows = occ_rows * groups
    per_dev = slots // plane
    width = coulomb_metric.shape[1]
    flat = (
        pair_tiles.reshape(slots, occ_rows, groups, LANES)
        .transpose(0, 2, 1, 3)
        .reshape(slots, tile_rows, LANES)
    )
    dma = pltpu.SemaphoreType.DMA
    out, pol = pl.pallas_call(
        functools.partial(fused_kernel, pairs, n_occ, slots),
        out_shape=(
            jax.ShapeDtypeStruct((slots, tile_rows, LANES), jnp.bfloat16),
            jax.ShapeDtypeStruct((per_dev * merged // LANES, LANES), jnp.float32),
        ),
        in_specs=[
            pl.BlockSpec(memory_space=pltpu.HBM),
            pl.BlockSpec(memory_space=pltpu.HBM),
            pl.BlockSpec(memory_space=pltpu.HBM),
            pl.BlockSpec(memory_space=pltpu.HBM),
        ],
        out_specs=(
            pl.BlockSpec(memory_space=pl.ANY),
            pl.BlockSpec(memory_space=pltpu.VMEM),
        ),
        scratch_shapes=[
            pltpu.VMEM((pairs, n_occ, 2, PBD, width // LANES, BLK, LANES), jnp.bfloat16),
            pltpu.VMEM((slots, tile_rows, LANES), jnp.bfloat16),
            pltpu.VMEM((slots, tile_rows, LANES), jnp.bfloat16),
            pltpu.VMEM((plane, per_dev // 2, BLK, LANES), jnp.bfloat16),
            pltpu.VMEM((plane - 1, per_dev // 2, BLK, LANES), jnp.bfloat16),
            pltpu.VMEM((per_dev // 2 * BLK, LANES), jnp.float32),
            pltpu.SMEM((2, slots), jnp.int32),
            pltpu.SMEM(owner_blocks.shape, jnp.int32),
            pltpu.SMEM((slots,), jnp.int32),
            pltpu.SMEM((slots,), jnp.int32),
            dma((PBD, width // LANES)),
            dma,
            dma((2,)),
            dma((plane,)),
            dma((pairs,)),
            dma((pairs,)),
            dma((pairs, CHUNKS)),
            dma,
            dma((pairs, CHUNKS)),
            dma,
            dma,
            dma((plane - 1,)),
            dma((plane - 1,)),
        ],
        compiler_params=pltpu.CompilerParams(
            collective_id=0, has_side_effects=True, vmem_limit_bytes=32 << 20
        ),
    )(block_list.T, owner_blocks, flat, coulomb_metric)
    contracted = (
        out.reshape(slots, groups, occ_rows, LANES)
        .transpose(0, 2, 1, 3)
        .reshape(slots, occ_rows, merged)
    )
    return contracted, pol.reshape(per_dev, merged)


def per_device(pair_tiles, block_list, owner_blocks, coulomb_metric):
    pairs = lax.axis_size("pair")
    plane = lax.axis_size("occ") * lax.axis_size("rep")
    gathered = coulomb_metric.size * 2 * pairs * plane
    if gathered <= GATHER_LIMIT and lax.axis_size("occ") == 2 and lax.axis_size("rep") == 2:
        return fused(pair_tiles, block_list, owner_blocks, coulomb_metric)
    return block_exchange(pair_tiles, block_list, owner_blocks, coulomb_metric)


def solution(mesh):
    placed = (
        P(("grp", "pair"), ("occ", "rep"), None),
        P(("grp", "pair"), None),
        P("grp", None),
        P(("grp", "pair"), ("occ", "rep")),
    )
    return jax.shard_map(
        per_device,
        mesh=mesh,
        in_specs=placed,
        out_specs=(
            P(("grp", "pair"), ("occ", "rep"), None),
            P(("grp", "pair", "occ", "rep"), None),
        ),
        check_vma=False,
    )
```

```python
import functools

import jax
import jax.numpy as jnp
from jax import lax
from jax.experimental import pallas as pl
from jax.experimental.pallas import tpu as pltpu
from jax.sharding import PartitionSpec as P

BLK = 64
PBD = 4
LANES = 128
MESH = pl.DeviceIdType.MESH
GATHER_LIMIT = 8 << 20
CHUNKS = 2


def block_exchange(pair_tiles, block_list, owner_blocks, coulomb_metric):
    slots, occ_rows = pair_tiles.shape[:2]
    rows = occ_rows * BLK
    pairs = lax.axis_size("pair")
    me = lax.axis_index("pair")
    capacity = max(2, 2 * slots // pairs)
    strip = lax.all_gather(coulomb_metric, ("occ", "rep"), axis=1, tiled=True)
    lists = lax.all_gather(block_list, "pair", axis=0, tiled=False)
    nu, aux = lists[:, :, 0], lists[:, :, 1]
    matched = (owner_blocks[None, None] == aux[:, :, None, None]).astype(jnp.int32)
    owner = jnp.sum(matched * jnp.arange(pairs, dtype=jnp.int32)[:, None], axis=(2, 3))
    local = jnp.sum(matched * jnp.arange(PBD, dtype=jnp.int32)[None, :], axis=(2, 3))
    position = jnp.arange(slots, dtype=jnp.int32)
    same_nu = (
        (nu[:, :, None] == nu[:, None, :]) & (position[:, None] != position[None, :])
    ).astype(jnp.int32)
    partner = jnp.sum(same_nu * position, axis=2)
    partner_aux = jnp.sum(same_nu * aux[:, None, :], axis=2)
    earlier = (owner[:, :, None] == owner[:, None, :]) & (position[None, :] < position[:, None])
    rank = jnp.sum(earlier.astype(jnp.int32), axis=2)
    chosen = (
        (owner == me)[:, None, :] & (rank[:, None, :] == jnp.arange(capacity)[None, :, None])
    ).astype(jnp.int32)
    send_local = jnp.sum(chosen * local[:, None, :], axis=2)
    send_aux = jnp.sum(chosen * aux[:, None, :], axis=2)
    send_partner = jnp.sum(chosen * partner_aux[:, None, :], axis=2)
    blocks = strip.reshape(PBD, BLK, -1, BLK).transpose(0, 2, 1, 3)
    send = jnp.stack([blocks[send_local, send_aux], blocks[send_local, send_partner]], axis=2)
    got = lax.all_to_all(send, "pair", split_axis=0, concat_axis=0, tiled=True)
    got = got.reshape(pairs * capacity, 2, BLK, BLK)
    mine = got[owner[me] * capacity + rank[me]]
    tiles = pair_tiles.reshape(slots, rows, BLK)
    products = jnp.einsum(
        "trc,tkcd->tkrd", tiles, mine, preferred_element_type=jnp.float32
    ).astype(jnp.bfloat16)
    total = products[:, 0].astype(jnp.float32) + products[partner[me], 1].astype(jnp.float32)
    rounded = total.astype(jnp.bfloat16)
    pol = jnp.einsum("srp,srq->spq", rounded, rounded, preferred_element_type=jnp.float32)
    pol = pol.reshape(slots, BLK * BLK).astype(jnp.bfloat16)
    pol = lax.psum_scatter(pol, ("occ", "rep"), scatter_dimension=0, tiled=True)
    return rounded.reshape(slots, occ_rows, BLK * BLK), pol.astype(jnp.float32)


def fused_kernel(
    pairs,
    n_occ,
    slots,
    lists_hbm,
    owners_hbm,
    tiles_hbm,
    metric_hbm,
    out_hbm,
    pol_ref,
    held,
    tiles,
    out,
    pol_send,
    pol_got,
    spread,
    lists,
    owners,
    place,
    mate,
    local_sem,
    tiles_sem,
    table_sem,
    out_sem,
    right_send,
    left_send,
    line_got,
    x_send,
    x_got,
    core_send,
    core_got,
    pol_out_sem,
    pol_in_sem,
):
    j = lax.axis_index("pair")
    occ = lax.axis_index("occ")
    rep = lax.axis_index("rep")
    plane = 2 * n_occ
    me = occ * 2 + rep
    halves = held.shape[4]
    part = PBD // CHUNKS
    per_dev = slots // plane
    packs = per_dev // 2
    other_x = {"occ": 1 - occ}
    other_core = {"rep": 1 - rep}
    other_both = {"occ": 1 - occ, "rep": 1 - rep}

    load_metric = [
        pltpu.make_async_copy(
            metric_hbm.at[k * BLK : (k + 1) * BLK, h * LANES : (h + 1) * LANES],
            held.at[j, occ, rep, k, h],
            local_sem.at[k, h],
        )
        for k in range(PBD)
        for h in range(halves)
    ]
    for copy in load_metric:
        copy.start()
    load_tiles = pltpu.make_async_copy(tiles_hbm, tiles, tiles_sem)
    load_tiles.start()
    load_lists = pltpu.make_async_copy(lists_hbm, lists, table_sem.at[0])
    load_lists.start()
    load_owners = pltpu.make_async_copy(owners_hbm, owners, table_sem.at[1])
    load_owners.start()

    barrier = pltpu.get_barrier_semaphore()

    def greet(device):
        pl.semaphore_signal(barrier, inc=1, device_id=device, device_id_type=MESH)

    greet(other_x)
    greet(other_core)
    greet(other_both)

    @pl.when(j > 0)
    def _():
        greet({"pair": j - 1})

    @pl.when(j < pairs - 1)
    def _():
        greet({"pair": j + 1})

    inner = (j > 0) & (j < pairs - 1)

    @pl.when(inner)
    def _():
        pl.semaphore_wait(barrier, 5)

    @pl.when(jnp.logical_not(inner))
    def _():
        pl.semaphore_wait(barrier, 4)


    def chunk(o, x, core, k):
        return held.at[o, x, core, pl.ds(k * part, part)]

    def right(o, k):
        c = chunk(o, occ, rep, k)
        return pltpu.make_async_remote_copy(
            c, c, right_send.at[o], line_got.at[o, k], {"pair": j + 1}, MESH
        )

    def left(o, k):
        c = chunk(o, occ, rep, k)
        return pltpu.make_async_remote_copy(
            c, c, left_send.at[o], line_got.at[o, k], {"pair": j - 1}, MESH
        )

    def across(o, k, x=occ):
        c = chunk(o, x, rep, k)
        return pltpu.make_async_remote_copy(c, c, x_send, x_got.at[o, k], other_x, MESH)

    def to_core(o, x, k):
        c = chunk(o, x, rep, k)
        return pltpu.make_async_remote_copy(c, c, core_send, core_got, other_core, MESH)

    for k in range(CHUNKS):
        for copy in load_metric[k * part * halves : (k + 1) * part * halves]:
            copy.wait()

        @pl.when(j < pairs - 1)
        def _(k=k):
            right(j, k).start()

        @pl.when(j > 0)
        def _(k=k):
            left(j, k).start()

        across(j, k).start()
    for k in range(CHUNKS):
        to_core(j, occ, k).start()

    def find(s, carry):
        aux = lists[1, s]
        nu = lists[0, s]
        where_ = jnp.int32(0)
        for k in range(pairs * PBD):
            where_ = jnp.where(owners[k // PBD, k % PBD] == aux, k, where_)
        place[s] = where_
        other = jnp.int32(0)
        for t in range(slots):
            other = jnp.where((lists[0, t] == nu) & (s != t), t, other)
        mate[s] = other
        return carry

    load_lists.wait()
    load_owners.wait()
    lax.fori_loop(0, slots, find, 0)

    def from_x(o, k):
        across(o, k, 1 - occ).wait_recv()
        to_core(o, 1 - occ, k).start()

    for d in range(1, pairs + 1):
        for k in range(CHUNKS):
            if d < pairs:
                lo, hi = j - d, j + d

                @pl.when(lo >= 0)
                def _(lo=lo, k=k):
                    right(lo, k).wait_recv()

                    @pl.when(j < pairs - 1)
                    def _():
                        right(lo, k).start()

                    across(lo, k).start()
                    to_core(lo, occ, k).start()

                @pl.when(hi < pairs)
                def _(hi=hi, k=k):
                    left(hi, k).wait_recv()

                    @pl.when(j > 0)
                    def _():
                        left(hi, k).start()

                    across(hi, k).start()
                    to_core(hi, occ, k).start()

            if d == 1:
                from_x(j, k)
            else:
                for o in (j - d + 1, j + d - 1):

                    @pl.when((o >= 0) & (o < pairs))
                    def _(o=o, k=k):
                        from_x(o, k)

    load_tiles.wait()

    theirs = held.at[:, :, 1 - rep]
    pltpu.make_async_remote_copy(theirs, theirs, core_send, core_got, other_core, MESH).wait_recv()

    lane = lax.broadcasted_iota(jnp.int32, (BLK, LANES), 1)
    low = lane < BLK

    def weights(row, col):
        half = col // 2
        dev = half // halves
        x = held[row // PBD, dev // 2, dev % 2, row % PBD, half % halves].astype(jnp.float32)
        turned = pltpu.roll(x, BLK, 1)
        even = jnp.full((BLK, LANES), col % 2, jnp.int32) == 0
        first = jnp.where(low, jnp.where(even, x, turned), 0.0)
        second = jnp.where(low, 0.0, jnp.where(even, turned, x))
        return jnp.concatenate([first, second], axis=0).astype(jnp.bfloat16)

    def contract(s):
        t = mate[s]
        col = lists[1, s]
        w = jnp.concatenate([weights(place[s], col), weights(place[t], col)], axis=0)
        a = jnp.concatenate([tiles[s], tiles[t]], axis=1)
        c = jnp.dot(a, w, preferred_element_type=jnp.float32).astype(jnp.bfloat16)
        out[s] = c
        return lax.dot_general(c, c, (((0,), (0,)), ((), ())), preferred_element_type=jnp.float32)

    def store_out(who, index):
        span = pl.ds(who * per_dev, per_dev)
        return pltpu.make_async_copy(out.at[span], out_hbm.at[span], out_sem.at[index])

    def send_pol(index, who, device):
        return pltpu.make_async_remote_copy(
            pol_send.at[who],
            pol_got.at[index],
            pol_out_sem.at[index],
            pol_in_sem.at[index],
            device,
            MESH,
        )

    routes = (
        (((1 - occ) * 2 + 1 - rep), other_both),
        (((1 - occ) * 2 + rep), other_x),
        ((occ * 2 + 1 - rep), other_core),
        (me, None),
    )
    for index, (who, device) in enumerate(routes):
        def pack(m, carry, who=who):
            s = who * per_dev + 2 * m
            g0 = contract(s)
            g1 = contract(s + 1)
            u = jnp.where(low, g0[:BLK], g1[BLK:])
            v = jnp.where(low, g1[:BLK], g0[BLK:])
            pol_send[who, m] = (u + pltpu.roll(v, BLK, 1)).astype(jnp.bfloat16)
            return carry

        lax.fori_loop(0, packs, pack, 0, unroll=True)
        if device is not None:
            send_pol(index, who, device).start()
        store_out(who, index).start()

    for index, (who, device) in enumerate(routes[:-1]):
        send_pol(index, who, device).wait()
    for m in range(packs):
        total = pol_send[me, m].astype(jnp.float32)
        for index in range(plane - 1):
            total = total + pol_got[index, m].astype(jnp.float32)
        spread[m * BLK : (m + 1) * BLK, :] = total
    even = spread[pl.ds(0, packs * BLK // 2, stride=2), :]
    odd = spread[pl.ds(1, packs * BLK // 2, stride=2), :]
    half = lax.broadcasted_iota(jnp.int32, even.shape, 1) < BLK
    first = jnp.where(half, even, pltpu.roll(odd, BLK, 1))
    second = jnp.where(half, pltpu.roll(even, BLK, 1), odd)
    rows = BLK // 2
    for m in range(packs):
        pol_ref[(2 * m) * rows : (2 * m + 1) * rows, :] = first[m * rows : (m + 1) * rows]
        pol_ref[(2 * m + 1) * rows : (2 * m + 2) * rows, :] = second[m * rows : (m + 1) * rows]
    for index, (who, _) in enumerate(routes):
        store_out(who, index).wait()

    mine = held.at[:, :, rep]
    pltpu.make_async_remote_copy(mine, mine, core_send, core_got, other_core, MESH).wait_send()
    column = held.at[:, occ, rep]
    pltpu.make_async_remote_copy(column, column, x_send, x_got.at[0, 0], other_x, MESH).wait_send()

    def settle(o, carry):
        block = held.at[o, occ, rep]

        @pl.when((o <= j) & (j < pairs - 1))
        def _():
            pltpu.make_async_remote_copy(
                block, block, right_send.at[o], line_got.at[o, 0], {"pair": j + 1}, MESH
            ).wait_send()

        @pl.when((o >= j) & (j > 0))
        def _():
            pltpu.make_async_remote_copy(
                block, block, left_send.at[o], line_got.at[o, 0], {"pair": j - 1}, MESH
            ).wait_send()

        return carry

    lax.fori_loop(0, pairs, settle, 0)


def fused(pair_tiles, block_list, owner_blocks, coulomb_metric):
    slots, occ_rows, merged = pair_tiles.shape
    pairs = lax.axis_size("pair")
    n_occ = lax.axis_size("occ")
    plane = n_occ * lax.axis_size("rep")
    groups = merged // LANES
    tile_rows = occ_rows * groups
    per_dev = slots // plane
    width = coulomb_metric.shape[1]
    flat = (
        pair_tiles.reshape(slots, occ_rows, groups, LANES)
        .transpose(0, 2, 1, 3)
        .reshape(slots, tile_rows, LANES)
    )
    dma = pltpu.SemaphoreType.DMA
    out, pol = pl.pallas_call(
        functools.partial(fused_kernel, pairs, n_occ, slots),
        out_shape=(
            jax.ShapeDtypeStruct((slots, tile_rows, LANES), jnp.bfloat16),
            jax.ShapeDtypeStruct((per_dev * merged // LANES, LANES), jnp.float32),
        ),
        in_specs=[
            pl.BlockSpec(memory_space=pltpu.HBM),
            pl.BlockSpec(memory_space=pltpu.HBM),
            pl.BlockSpec(memory_space=pltpu.HBM),
            pl.BlockSpec(memory_space=pltpu.HBM),
        ],
        out_specs=(
            pl.BlockSpec(memory_space=pl.ANY),
            pl.BlockSpec(memory_space=pltpu.VMEM),
        ),
        scratch_shapes=[
            pltpu.VMEM((pairs, n_occ, 2, PBD, width // LANES, BLK, LANES), jnp.bfloat16),
            pltpu.VMEM((slots, tile_rows, LANES), jnp.bfloat16),
            pltpu.VMEM((slots, tile_rows, LANES), jnp.bfloat16),
            pltpu.VMEM((plane, per_dev // 2, BLK, LANES), jnp.bfloat16),
            pltpu.VMEM((plane - 1, per_dev // 2, BLK, LANES), jnp.bfloat16),
            pltpu.VMEM((per_dev // 2 * BLK, LANES), jnp.float32),
            pltpu.SMEM((2, slots), jnp.int32),
            pltpu.SMEM(owner_blocks.shape, jnp.int32),
            pltpu.SMEM((slots,), jnp.int32),
            pltpu.SMEM((slots,), jnp.int32),
            dma((PBD, width // LANES)),
            dma,
            dma((2,)),
            dma((plane,)),
            dma((pairs,)),
            dma((pairs,)),
            dma((pairs, CHUNKS)),
            dma,
            dma((pairs, CHUNKS)),
            dma,
            dma,
            dma((plane - 1,)),
            dma((plane - 1,)),
        ],
        compiler_params=pltpu.CompilerParams(
            collective_id=0, has_side_effects=True, vmem_limit_bytes=32 << 20
        ),
    )(block_list.T, owner_blocks, flat, coulomb_metric)
    contracted = (
        out.reshape(slots, groups, occ_rows, LANES)
        .transpose(0, 2, 1, 3)
        .reshape(slots, occ_rows, merged)
    )
    return contracted, pol.reshape(per_dev, merged)


def per_device(pair_tiles, block_list, owner_blocks, coulomb_metric):
    pairs = lax.axis_size("pair")
    plane = lax.axis_size("occ") * lax.axis_size("rep")
    gathered = coulomb_metric.size * 2 * pairs * plane
    if gathered <= GATHER_LIMIT and lax.axis_size("occ") == 2 and lax.axis_size("rep") == 2:
        return fused(pair_tiles, block_list, owner_blocks, coulomb_metric)
    return block_exchange(pair_tiles, block_list, owner_blocks, coulomb_metric)


def solution(mesh):
    placed = (
        P(("grp", "pair"), ("occ", "rep"), None),
        P(("grp", "pair"), None),
        P("grp", None),
        P(("grp", "pair"), ("occ", "rep")),
    )
    return jax.shard_map(
        per_device,
        mesh=mesh,
        in_specs=placed,
        out_specs=(
            P(("grp", "pair"), ("occ", "rep"), None),
            P(("grp", "pair", "occ", "rep"), None),
        ),
        check_vma=False,
    )
```

```python
import functools

import jax
import jax.numpy as jnp
from jax import lax
from jax.experimental import pallas as pl
from jax.experimental.pallas import tpu as pltpu
from jax.sharding import PartitionSpec as P

BLK = 64
PBD = 4
LANES = 128
MESH = pl.DeviceIdType.MESH
GATHER_LIMIT = 8 << 20
CHUNKS = 2


def block_exchange(pair_tiles, block_list, owner_blocks, coulomb_metric):
    slots, occ_rows = pair_tiles.shape[:2]
    rows = occ_rows * BLK
    pairs = lax.axis_size("pair")
    me = lax.axis_index("pair")
    capacity = max(2, 2 * slots // pairs)
    strip = lax.all_gather(coulomb_metric, ("occ", "rep"), axis=1, tiled=True)
    lists = lax.all_gather(block_list, "pair", axis=0, tiled=False)
    nu, aux = lists[:, :, 0], lists[:, :, 1]
    matched = (owner_blocks[None, None] == aux[:, :, None, None]).astype(jnp.int32)
    owner = jnp.sum(matched * jnp.arange(pairs, dtype=jnp.int32)[:, None], axis=(2, 3))
    local = jnp.sum(matched * jnp.arange(PBD, dtype=jnp.int32)[None, :], axis=(2, 3))
    position = jnp.arange(slots, dtype=jnp.int32)
    same_nu = (
        (nu[:, :, None] == nu[:, None, :]) & (position[:, None] != position[None, :])
    ).astype(jnp.int32)
    partner = jnp.sum(same_nu * position, axis=2)
    partner_aux = jnp.sum(same_nu * aux[:, None, :], axis=2)
    earlier = (owner[:, :, None] == owner[:, None, :]) & (position[None, :] < position[:, None])
    rank = jnp.sum(earlier.astype(jnp.int32), axis=2)
    chosen = (
        (owner == me)[:, None, :] & (rank[:, None, :] == jnp.arange(capacity)[None, :, None])
    ).astype(jnp.int32)
    send_local = jnp.sum(chosen * local[:, None, :], axis=2)
    send_aux = jnp.sum(chosen * aux[:, None, :], axis=2)
    send_partner = jnp.sum(chosen * partner_aux[:, None, :], axis=2)
    blocks = strip.reshape(PBD, BLK, -1, BLK).transpose(0, 2, 1, 3)
    send = jnp.stack([blocks[send_local, send_aux], blocks[send_local, send_partner]], axis=2)
    got = lax.all_to_all(send, "pair", split_axis=0, concat_axis=0, tiled=True)
    got = got.reshape(pairs * capacity, 2, BLK, BLK)
    mine = got[owner[me] * capacity + rank[me]]
    tiles = pair_tiles.reshape(slots, rows, BLK)
    products = jnp.einsum(
        "trc,tkcd->tkrd", tiles, mine, preferred_element_type=jnp.float32
    ).astype(jnp.bfloat16)
    total = products[:, 0].astype(jnp.float32) + products[partner[me], 1].astype(jnp.float32)
    rounded = total.astype(jnp.bfloat16)
    pol = jnp.einsum("srp,srq->spq", rounded, rounded, preferred_element_type=jnp.float32)
    pol = pol.reshape(slots, BLK * BLK).astype(jnp.bfloat16)
    pol = lax.psum_scatter(pol, ("occ", "rep"), scatter_dimension=0, tiled=True)
    return rounded.reshape(slots, occ_rows, BLK * BLK), pol.astype(jnp.float32)


def fused_kernel(
    pairs,
    n_occ,
    slots,
    lists_hbm,
    owners_hbm,
    tiles_hbm,
    metric_hbm,
    out_hbm,
    pol_ref,
    held,
    tiles,
    out,
    pol_send,
    pol_got,
    spread,
    lists,
    owners,
    place,
    mate,
    local_sem,
    tiles_sem,
    table_sem,
    out_sem,
    right_send,
    left_send,
    line_got,
    x_send,
    x_got,
    core_send,
    core_got,
    pol_out_sem,
    pol_in_sem,
):
    j = lax.axis_index("pair")
    occ = lax.axis_index("occ")
    rep = lax.axis_index("rep")
    plane = 2 * n_occ
    me = occ * 2 + rep
    halves = held.shape[4]
    part = PBD // CHUNKS
    per_dev = slots // plane
    packs = per_dev // 2
    other_x = {"occ": 1 - occ}
    other_core = {"rep": 1 - rep}
    other_both = {"occ": 1 - occ, "rep": 1 - rep}

    load_metric = [
        pltpu.make_async_copy(
            metric_hbm.at[k * BLK : (k + 1) * BLK, h * LANES : (h + 1) * LANES],
            held.at[j, occ, rep, k, h],
            local_sem.at[k, h],
        )
        for k in range(PBD)
        for h in range(halves)
    ]
    for copy in load_metric:
        copy.start()
    load_tiles = pltpu.make_async_copy(tiles_hbm, tiles, tiles_sem)
    load_tiles.start()
    load_lists = pltpu.make_async_copy(lists_hbm, lists, table_sem.at[0])
    load_lists.start()
    load_owners = pltpu.make_async_copy(owners_hbm, owners, table_sem.at[1])
    load_owners.start()

    barrier = pltpu.get_barrier_semaphore()

    def greet(device):
        pl.semaphore_signal(barrier, inc=1, device_id=device, device_id_type=MESH)

    greet(other_x)
    greet(other_core)
    greet(other_both)

    @pl.when(j > 0)
    def _():
        greet({"pair": j - 1})

    @pl.when(j < pairs - 1)
    def _():
        greet({"pair": j + 1})

    inner = (j > 0) & (j < pairs - 1)

    @pl.when(inner)
    def _():
        pl.semaphore_wait(barrier, 5)

    @pl.when(jnp.logical_not(inner))
    def _():
        pl.semaphore_wait(barrier, 4)


    def chunk(o, x, core, k):
        return held.at[o, x, core, pl.ds(k * part, part)]

    def right(o, k):
        c = chunk(o, occ, rep, k)
        return pltpu.make_async_remote_copy(
            c, c, right_send.at[o], line_got.at[o, k], {"pair": j + 1}, MESH
        )

    def left(o, k):
        c = chunk(o, occ, rep, k)
        return pltpu.make_async_remote_copy(
            c, c, left_send.at[o], line_got.at[o, k], {"pair": j - 1}, MESH
        )

    def across(o, k, x=occ):
        c = chunk(o, x, rep, k)
        return pltpu.make_async_remote_copy(c, c, x_send, x_got.at[o, k], other_x, MESH)

    def to_core(o, x, k):
        c = chunk(o, x, rep, k)
        return pltpu.make_async_remote_copy(c, c, core_send, core_got, other_core, MESH)

    for k in range(CHUNKS):
        for copy in load_metric[k * part * halves : (k + 1) * part * halves]:
            copy.wait()

        @pl.when(j < pairs - 1)
        def _(k=k):
            right(j, k).start()

        @pl.when(j > 0)
        def _(k=k):
            left(j, k).start()

        across(j, k).start()
    for k in range(CHUNKS):
        to_core(j, occ, k).start()

    def find(s, carry):
        aux = lists[1, s]
        nu = lists[0, s]
        where_ = jnp.int32(0)
        for k in range(pairs * PBD):
            where_ = jnp.where(owners[k // PBD, k % PBD] == aux, k, where_)
        place[s] = where_
        other = jnp.int32(0)
        for t in range(slots):
            other = jnp.where((lists[0, t] == nu) & (s != t), t, other)
        mate[s] = other
        return carry

    load_lists.wait()
    load_owners.wait()
    lax.fori_loop(0, slots, find, 0)

    def from_x(o, k):
        across(o, k, 1 - occ).wait_recv()
        to_core(o, 1 - occ, k).start()

    for d in range(1, pairs + 1):
        for k in range(CHUNKS):
            if d < pairs:
                lo, hi = j - d, j + d

                @pl.when(lo >= 0)
                def _(lo=lo, k=k):
                    right(lo, k).wait_recv()

                    @pl.when(j < pairs - 1)
                    def _():
                        right(lo, k).start()

                    across(lo, k).start()
                    to_core(lo, occ, k).start()

                @pl.when(hi < pairs)
                def _(hi=hi, k=k):
                    left(hi, k).wait_recv()

                    @pl.when(j > 0)
                    def _():
                        left(hi, k).start()

                    across(hi, k).start()
                    to_core(hi, occ, k).start()

            if d == 1:
                from_x(j, k)
            else:
                for o in (j - d + 1, j + d - 1):

                    @pl.when((o >= 0) & (o < pairs))
                    def _(o=o, k=k):
                        from_x(o, k)

    load_tiles.wait()

    theirs = held.at[:, :, 1 - rep]
    pltpu.make_async_remote_copy(theirs, theirs, core_send, core_got, other_core, MESH).wait_recv()

    lane = lax.broadcasted_iota(jnp.int32, (BLK, LANES), 1)
    low = lane < BLK

    def weights(row, col):
        half = col // 2
        dev = half // halves
        x = held[row // PBD, dev // 2, dev % 2, row % PBD, half % halves].astype(jnp.float32)
        turned = pltpu.roll(x, BLK, 1)
        even = jnp.full((BLK, LANES), col % 2, jnp.int32) == 0
        first = jnp.where(low, jnp.where(even, x, turned), 0.0)
        second = jnp.where(low, 0.0, jnp.where(even, turned, x))
        return jnp.concatenate([first, second], axis=0).astype(jnp.bfloat16)

    def contract(s):
        t = mate[s]
        col = lists[1, s]
        w = jnp.concatenate([weights(place[s], col), weights(place[t], col)], axis=0)
        a = jnp.concatenate([tiles[s], tiles[t]], axis=1)
        c = jnp.dot(a, w, preferred_element_type=jnp.float32).astype(jnp.bfloat16)
        out[s] = c
        return lax.dot_general(c, c, (((0,), (0,)), ((), ())), preferred_element_type=jnp.float32)

    def store_out(who, index):
        span = pl.ds(who * per_dev, per_dev)
        return pltpu.make_async_copy(out.at[span], out_hbm.at[span], out_sem.at[index])

    def send_pol(index, who, device):
        return pltpu.make_async_remote_copy(
            pol_send.at[who],
            pol_got.at[index],
            pol_out_sem.at[index],
            pol_in_sem.at[index],
            device,
            MESH,
        )

    routes = (
        (((1 - occ) * 2 + 1 - rep), other_both),
        (((1 - occ) * 2 + rep), other_x),
        ((occ * 2 + 1 - rep), other_core),
        (me, None),
    )
    for index, (who, device) in enumerate(routes):
        def pack(m, carry, who=who):
            s = who * per_dev + 2 * m
            g0 = contract(s)
            g1 = contract(s + 1)
            u = jnp.where(low, g0[:BLK], g1[BLK:])
            v = jnp.where(low, g1[:BLK], g0[BLK:])
            pol_send[who, m] = (u + pltpu.roll(v, BLK, 1)).astype(jnp.bfloat16)
            return carry

        lax.fori_loop(0, packs, pack, 0, unroll=True)
        if device is not None:
            send_pol(index, who, device).start()
        store_out(who, index).start()

    for index, (who, device) in enumerate(routes[:-1]):
        send_pol(index, who, device).wait()
    for m in range(packs):
        total = pol_send[me, m].astype(jnp.float32)
        for index in range(plane - 1):
            total = total + pol_got[index, m].astype(jnp.float32)
        spread[m * BLK : (m + 1) * BLK, :] = total
    even = spread[pl.ds(0, packs * BLK // 2, stride=2), :]
    odd = spread[pl.ds(1, packs * BLK // 2, stride=2), :]
    half = lax.broadcasted_iota(jnp.int32, even.shape, 1) < BLK
    first = jnp.where(half, even, pltpu.roll(odd, BLK, 1))
    second = jnp.where(half, pltpu.roll(even, BLK, 1), odd)
    rows = BLK // 2
    for m in range(packs):
        pol_ref[(2 * m) * rows : (2 * m + 1) * rows, :] = first[m * rows : (m + 1) * rows]
        pol_ref[(2 * m + 1) * rows : (2 * m + 2) * rows, :] = second[m * rows : (m + 1) * rows]
    for index, (who, _) in enumerate(routes):
        store_out(who, index).wait()

    mine = held.at[:, :, rep]
    pltpu.make_async_remote_copy(mine, mine, core_send, core_got, other_core, MESH).wait_send()
    column = held.at[:, occ, rep]
    pltpu.make_async_remote_copy(column, column, x_send, x_got.at[0, 0], other_x, MESH).wait_send()

    def settle(o, carry):
        block = held.at[o, occ, rep]

        @pl.when((o <= j) & (j < pairs - 1))
        def _():
            pltpu.make_async_remote_copy(
                block, block, right_send.at[o], line_got.at[o, 0], {"pair": j + 1}, MESH
            ).wait_send()

        @pl.when((o >= j) & (j > 0))
        def _():
            pltpu.make_async_remote_copy(
                block, block, left_send.at[o], line_got.at[o, 0], {"pair": j - 1}, MESH
            ).wait_send()

        return carry

    lax.fori_loop(0, pairs, settle, 0)


def fused(pair_tiles, block_list, owner_blocks, coulomb_metric):
    slots, occ_rows, merged = pair_tiles.shape
    pairs = lax.axis_size("pair")
    n_occ = lax.axis_size("occ")
    plane = n_occ * lax.axis_size("rep")
    groups = merged // LANES
    tile_rows = occ_rows * groups
    per_dev = slots // plane
    width = coulomb_metric.shape[1]
    flat = (
        pair_tiles.reshape(slots, occ_rows, groups, LANES)
        .transpose(0, 2, 1, 3)
        .reshape(slots, tile_rows, LANES)
    )
    dma = pltpu.SemaphoreType.DMA
    out, pol = pl.pallas_call(
        functools.partial(fused_kernel, pairs, n_occ, slots),
        out_shape=(
            jax.ShapeDtypeStruct((slots, tile_rows, LANES), jnp.bfloat16),
            jax.ShapeDtypeStruct((per_dev * merged // LANES, LANES), jnp.float32),
        ),
        in_specs=[
            pl.BlockSpec(memory_space=pltpu.HBM),
            pl.BlockSpec(memory_space=pltpu.HBM),
            pl.BlockSpec(memory_space=pltpu.HBM),
            pl.BlockSpec(memory_space=pltpu.HBM),
        ],
        out_specs=(
            pl.BlockSpec(memory_space=pl.ANY),
            pl.BlockSpec(memory_space=pltpu.VMEM),
        ),
        scratch_shapes=[
            pltpu.VMEM((pairs, n_occ, 2, PBD, width // LANES, BLK, LANES), jnp.bfloat16),
            pltpu.VMEM((slots, tile_rows, LANES), jnp.bfloat16),
            pltpu.VMEM((slots, tile_rows, LANES), jnp.bfloat16),
            pltpu.VMEM((plane, per_dev // 2, BLK, LANES), jnp.bfloat16),
            pltpu.VMEM((plane - 1, per_dev // 2, BLK, LANES), jnp.bfloat16),
            pltpu.VMEM((per_dev // 2 * BLK, LANES), jnp.float32),
            pltpu.SMEM((2, slots), jnp.int32),
            pltpu.SMEM(owner_blocks.shape, jnp.int32),
            pltpu.SMEM((slots,), jnp.int32),
            pltpu.SMEM((slots,), jnp.int32),
            dma((PBD, width // LANES)),
            dma,
            dma((2,)),
            dma((plane,)),
            dma((pairs,)),
            dma((pairs,)),
            dma((pairs, CHUNKS)),
            dma,
            dma((pairs, CHUNKS)),
            dma,
            dma,
            dma((plane - 1,)),
            dma((plane - 1,)),
        ],
        compiler_params=pltpu.CompilerParams(
            collective_id=0, has_side_effects=True, vmem_limit_bytes=105 << 19
        ),
    )(block_list.T, owner_blocks, flat, coulomb_metric)
    contracted = (
        out.reshape(slots, groups, occ_rows, LANES)
        .transpose(0, 2, 1, 3)
        .reshape(slots, occ_rows, merged)
    )
    return contracted, pol.reshape(per_dev, merged)


def per_device(pair_tiles, block_list, owner_blocks, coulomb_metric):
    pairs = lax.axis_size("pair")
    plane = lax.axis_size("occ") * lax.axis_size("rep")
    gathered = coulomb_metric.size * 2 * pairs * plane
    if gathered <= GATHER_LIMIT and lax.axis_size("occ") == 2 and lax.axis_size("rep") == 2:
        return fused(pair_tiles, block_list, owner_blocks, coulomb_metric)
    return block_exchange(pair_tiles, block_list, owner_blocks, coulomb_metric)


def solution(mesh):
    placed = (
        P(("grp", "pair"), ("occ", "rep"), None),
        P(("grp", "pair"), None),
        P("grp", None),
        P(("grp", "pair"), ("occ", "rep")),
    )
    return jax.shard_map(
        per_device,
        mesh=mesh,
        in_specs=placed,
        out_specs=(
            P(("grp", "pair"), ("occ", "rep"), None),
            P(("grp", "pair", "occ", "rep"), None),
        ),
        check_vma=False,
    )
```
